32 devices in a mesh: wide: 8 (over z, y), narrow: 4 (over x, core).
Axes of the slice: x: 2, y: 2, z: 4, core: 2. Of those that a mesh axis runs over, the one named last changes fastest.
Arguments:
- amplitudes: bfloat16 [512, 8, 4096], P('narrow', 'wide'), may hold values from -6 to 6
- integrals: bfloat16 [8, 2, 4096, 4096], P('wide', None, None, 'narrow'), may hold values from -0.09375 to 0.09375
- targets: int32 [8, 2], replicated, may hold values from 0 to 7, as said below
- counts: int32 [8], replicated, may hold values from 1 to 2, as said below
Outputs:
- residual: float32 [512, 8, 4096], P('wide', None, 'narrow')
The draws below stay inside these ranges and needn't reach their ends.
Inputs may be any that keep to these rules, and one draw needn't show every extreme that they name: `targets`: the 2 entries of one row are different pair tiles. `counts`: every panel holds at least one block.
All inputs are finite; a program needn't handle non-finite values.
Results may differ from the reference program's by a relative error of at most 0.0003.
Values may be sent and summed in bfloat16 or wider, within the bound.
No kernel may reach another device: no remote copies, remote signals or barrier semaphores. Data moves between devices by JAX's collectives and lax.ppermute only.
A program may use at most 64 MiB of HBM per device.

```python
import jax
import jax.numpy as jnp
from jax import lax

PAIR = 4096
IJ = 512
SLOTS = 2
PAIRS = 8


def draw_targets(key, part):
    key_base = jax.random.fold_in(key, 11)
    key_stride = jax.random.fold_in(key, 12)
    key_first = jax.random.fold_in(key, 13)
    key_second = jax.random.fold_in(key, 14)
    base_tile = jax.random.randint(key_base, (PAIRS,), 0, PAIRS, dtype=jnp.int32)
    stride_tile = jax.random.randint(key_stride, (PAIRS,), 1, PAIRS // SLOTS + 1, dtype=jnp.int32)
    first_row = jax.random.randint(key_first, (), 0, PAIRS, dtype=jnp.int32)
    second_row = (first_row + 1 + jax.random.randint(key_second, (), 0, PAIRS - 1, dtype=jnp.int32)) % PAIRS
    base_tile = base_tile.at[first_row].set(0)
    base_tile = base_tile.at[second_row].set(PAIRS - 1)
    slot_ids = jnp.arange(SLOTS, dtype=jnp.int32)
    return ((base_tile[:, None] + slot_ids[None, :] * stride_tile[:, None]) % PAIRS).astype(jnp.int32)


def draw_counts(key, part):
    key_count = jax.random.fold_in(key, 21)
    key_first = jax.random.fold_in(key, 22)
    key_second = jax.random.fold_in(key, 23)
    task_count = jax.random.randint(key_count, (PAIRS,), 1, SLOTS + 1, dtype=jnp.int32)
    first_row = jax.random.randint(key_first, (), 0, PAIRS, dtype=jnp.int32)
    second_row = (first_row + 1 + jax.random.randint(key_second, (), 0, PAIRS - 1, dtype=jnp.int32)) % PAIRS
    task_count = task_count.at[first_row].set(SLOTS)
    task_count = task_count.at[second_row].set(1)
    return task_count.astype(jnp.int32)


def block_scale(rng, shape, split, least, largest):
    level, own = 1.0, jax.random.fold_in(rng, 6)
    for position, blocks in split:
        draws = jnp.exp(jax.random.uniform(jax.random.fold_in(own, position), (blocks,), jnp.float32, least / len(split), largest / len(split)))
        level = level * jnp.repeat(draws, shape[position] // blocks).reshape([-1 if axis == position else 1 for axis in range(len(shape))])
    return level


def noise(stream_key, shape, deviation, reach, shards=(), kind=jnp.bfloat16):
    loudness = block_scale(stream_key, shape, shards, -0.22, 0.18) if shards else 1.0
    result = jax.random.normal(stream_key, shape, jnp.float32) * deviation * loudness
    return jnp.minimum(jnp.maximum(result, -reach), reach).astype(kind)


def setup_inputs(seed: int = 0) -> dict:
    seeds = jax.random.split(jax.random.key(seed), 5)
    return {
        "amplitudes": noise(seeds[0], (IJ, PAIRS, PAIR), 1.0, 6.0, ((0, 4), (1, 8))),
        "integrals": noise(seeds[1], (PAIRS, SLOTS, PAIR, PAIR), PAIR ** -0.5, 0.09375, ((0, 8), (3, 4))),
        "targets": draw_targets(jax.random.fold_in(seeds[4], 71), 0),
        "counts": draw_counts(jax.random.fold_in(seeds[4], 71), 0),
    }


def reference(amplitudes, integrals, targets, counts):
    total = jnp.zeros((amplitudes.shape[0], PAIRS, amplitudes.shape[2]), jnp.float32)

    def panel_step(current_total, panel_index):
        panel_rows = lax.dynamic_index_in_dim(amplitudes, panel_index, 1, keepdims=False)
        panel_blocks = lax.dynamic_index_in_dim(integrals, panel_index, 0, keepdims=False)
        target_row = lax.dynamic_index_in_dim(targets, panel_index, 0, keepdims=False)
        live_count = lax.dynamic_index_in_dim(counts, panel_index, 0, keepdims=False)
        for slot_index in range(SLOTS):
            integral_block = panel_blocks[slot_index]
            target_tile = target_row[slot_index].astype(jnp.int32)

            def add_block(running, integral_block=integral_block, target_tile=target_tile):
                product = jnp.dot(panel_rows, integral_block, preferred_element_type=jnp.float32)
                column = lax.dynamic_index_in_dim(running, target_tile, 1, keepdims=False) + product
                return lax.dynamic_update_index_in_dim(running, column, target_tile, 1)

            def keep_block(running):
                return running

            current_total = lax.cond(slot_index < live_count, add_block, keep_block, current_total)
        return current_total, None

    total, unused_output = lax.scan(panel_step, total, jnp.arange(PAIRS, dtype=jnp.int32))
    return total
```

```python
import functools

import jax
import jax.numpy as jnp
from jax import lax
from jax.experimental import pallas as pl
from jax.experimental.pallas import tpu as pltpu
from jax.sharding import PartitionSpec as P

MIB = 1 << 20
TOP = 32766.0
MANT = 8192.0
MODES = ("direct", "direct")


def scale_code(peak):
    exponent = jnp.clip(jnp.floor(jnp.log2(jnp.maximum(peak, 1e-37))), -125.0, 125.0)
    mantissa = jnp.minimum(jnp.ceil(peak * jnp.exp2(-exponent) * MANT) + 1.0, 32000.0)
    return exponent, jnp.maximum(mantissa, 1.0)


def stage_kernel(source, kept, done):
    copy = pltpu.make_async_copy(source, kept, done)
    copy.start()
    copy.wait()


def staged(integrals):
    return pl.pallas_call(
        stage_kernel,
        out_shape=pltpu.VMEM(integrals.shape, integrals.dtype),
        in_specs=[pl.BlockSpec(memory_space=pltpu.HBM)],
        out_specs=pl.BlockSpec(memory_space=pltpu.VMEM),
        scratch_shapes=[pltpu.SemaphoreType.DMA],
        compiler_params=pltpu.CompilerParams(vmem_limit_bytes=40 * MIB),
        name="staged_integrals",
    )(integrals)


def pick_kernel(source, *refs):
    refs[-1][...] = source[...]


def picked(own, start, rows, after):
    share, _, depth = own.shape
    return pl.pallas_call(
        pick_kernel,
        out_shape=jax.ShapeDtypeStruct((share, rows, depth), own.dtype),
        grid=(1,),
        in_specs=[pl.BlockSpec((share, rows, depth), lambda i: (0, start // rows, 0))]
        + [pl.BlockSpec(memory_space=pl.ANY)] * len(after),
        out_specs=pl.BlockSpec((share, rows, depth), lambda i: (0, 0, 0)),
        compiler_params=pltpu.CompilerParams(vmem_limit_bytes=8 * MIB),
        name="picked_rows",
    )(own, *after)


def product_kernel(slots, wide, narrow, share, rows, joint, ids, *refs):
    pieces, block = refs[:narrow], refs[narrow]
    outs = refs[narrow + 1 : -3]
    left, total, codes = refs[-3:]
    me, mine = ids[0], ids[1]
    cols = block.shape[3]
    groups, lanes = rows // 16, cols // 128
    tiles = slots * groups * lanes + 1
    for k in range(narrow):
        for sub in range(share):
            place = ((mine ^ k) * share + sub) ^ me
            left[pl.ds(pl.multiple_of(place * rows, rows), rows), :] = pieces[k][sub]
    codes[...] = jnp.zeros_like(codes)
    lane = lax.broadcasted_iota(jnp.int32, (16, 128), 1)

    def one_slot(slot, carry):
        for n in range(cols // 256):
            span = slice(n * 256, n * 256 + 256)
            total[:, span] = jnp.dot(left[...], block[0, slot, :, span], preferred_element_type=jnp.float32)
        for s in range(wide):
            for g in range(groups):
                value = total[s * rows + g * 16 : s * rows + g * 16 + 16, :]
                peak = jnp.max(jnp.abs(value), axis=1, keepdims=True)
                exponent, mantissa = scale_code(peak)
                value = value * jnp.exp2(-exponent) * (TOP * MANT / mantissa)
                value = jnp.round(value).astype(jnp.int32).astype(jnp.int16)
                at = (s % joint) * tiles + (slot * groups + g) * lanes
                for t in range(lanes):
                    outs[s // joint][at + t] = value[:, t * 128 : t * 128 + 128]
                spot = (slot * groups + g) * 2
                code = jnp.where(lane == spot, exponent.astype(jnp.int32), codes[s])
                codes[s] = jnp.where(lane == spot + 1, mantissa.astype(jnp.int32), code)
        return carry

    lax.fori_loop(0, slots, one_slot, 0)
    for s in range(wide):
        outs[s // joint][(s % joint) * tiles + tiles - 1] = codes[s].astype(jnp.int16)


def products(ids, pieces, integrals, wide, joint):
    _, slots, depth, cols = integrals.shape
    narrow = len(pieces)
    share, rows, _ = pieces[0].shape
    tiles = slots * (rows // 16) * (cols // 128) + 1
    vmem = pl.BlockSpec(memory_space=pltpu.VMEM)
    return pl.pallas_call(
        functools.partial(product_kernel, slots, wide, narrow, share, rows, joint),
        out_shape=[jax.ShapeDtypeStruct((joint * tiles, 16, 128), jnp.int16)] * (wide // joint),
        in_specs=[pl.BlockSpec(memory_space=pltpu.SMEM)] + [vmem] * (narrow + 1),
        out_specs=[vmem] * (wide // joint),
        scratch_shapes=[
            pltpu.VMEM((wide * rows, depth), jnp.bfloat16),
            pltpu.VMEM((wide * rows, cols), jnp.float32),
            pltpu.VMEM((wide, 16, 128), jnp.int32),
        ],
        compiler_params=pltpu.CompilerParams(vmem_limit_bytes=16 * MIB),
        cost_estimate=pl.CostEstimate(
            flops=16 * slots * wide * rows * depth * cols,
            bytes_accessed=2 * wide * rows * depth,
            transcendentals=0,
        ),
        name="products",
    )(ids, *pieces, integrals)


def sum_kernel(slots, plan, rows, cols, ids, targets, counts, *refs):
    out, total = refs[-2:]
    me = ids[0]
    groups, lanes = rows // 16, cols // 128
    tiles = slots * groups * lanes + 1
    total[...] = jnp.zeros_like(total)
    lane = lax.broadcasted_iota(jnp.int32, (16, 128), 1)
    for index, bits, at in plan:
        panel = me ^ bits
        codes = refs[index][at + tiles - 1].astype(jnp.int32)
        for j in range(slots):

            @pl.when(j < counts[panel])
            def add():
                tile = targets[panel * slots + j]
                for g in range(groups):
                    spot = (j * groups + g) * 2
                    exponent = jnp.sum(jnp.where(lane == spot, codes, 0).astype(jnp.float32), axis=1, keepdims=True)
                    mantissa = jnp.sum(jnp.where(lane == spot + 1, codes, 0).astype(jnp.float32), axis=1, keepdims=True)
                    scale = jnp.exp2(exponent) * (mantissa * (1.0 / (TOP * MANT)))
                    for t in range(lanes):
                        value = refs[index][at + (j * groups + g) * lanes + t].astype(jnp.int32).astype(jnp.float32)
                        total[tile, g * 16 : g * 16 + 16, t * 128 : t * 128 + 128] += value * scale
    for g in range(rows // 8):
        for t in range(lanes):
            span = slice(t * 128, t * 128 + 128)
            out[g * 8 : g * 8 + 8, :, span] = jnp.swapaxes(total[:, g * 8 : g * 8 + 8, span], 0, 1)


def summed(ids, targets, counts, given, plan, held, start, rows, cols, height):
    pairs, slots = targets.shape
    extra = [] if held is None else [held]
    return pl.pallas_call(
        functools.partial(sum_kernel, slots, plan, rows, cols),
        out_shape=jax.ShapeDtypeStruct((height, pairs, cols), jnp.float32),
        grid_spec=pltpu.PrefetchScalarGridSpec(
            num_scalar_prefetch=3,
            grid=(1,),
            in_specs=[pl.BlockSpec(g.shape, lambda i, *_: (0, 0, 0)) for g in given]
            + [pl.BlockSpec(memory_space=pl.ANY)] * len(extra),
            out_specs=pl.BlockSpec((rows, pairs, cols), lambda i, *_: (start // rows, 0, 0)),
            scratch_shapes=[pltpu.VMEM((pairs, rows, cols), jnp.float32)],
        ),
        input_output_aliases={3 + len(given): 0} if extra else {},
        compiler_params=pltpu.CompilerParams(vmem_limit_bytes=32 * MIB),
        cost_estimate=pl.CostEstimate(
            flops=4 * pairs * slots * rows * cols,
            bytes_accessed=2 * pairs * slots * rows * cols + 4 * pairs * rows * cols,
            transcendentals=0,
        ),
        name="tile_sums",
    )(ids, targets.reshape(-1), counts, *given, *extra)


def on_device(amplitudes, integrals, targets, counts):
    wide, narrow = lax.axis_size("wide"), lax.axis_size("narrow")
    me, mine = lax.axis_index("wide"), lax.axis_index("narrow")
    ids = jnp.stack([me, mine]).astype(jnp.int32)
    depth, cols = integrals.shape[2], integrals.shape[3]
    share = wide // narrow
    height = amplitudes.shape[0] // share
    own = amplitudes.reshape(share, height, depth)
    parts = [16] * (height // 16) if height < 64 else [32, height - 32]

    def across(array, axis, size, bits):
        return lax.ppermute(array, axis, [(i, i ^ bits) for i in range(size)])

    starts = [sum(parts[:i]) for i in range(len(parts))]
    kept = staged(integrals)
    beside = across(own, "narrow", narrow, 1)
    received, arrivals, after, ready = [], [], [], [kept]
    for start, rows, mode in zip(starts, parts, MODES):
        chunk = picked(own, start, rows, after)
        far = [across(chunk, "narrow", narrow, k) for k in range(2, narrow, 2)]
        after = far[-1:]
        far = [picked(c, 0, rows, ready) if ready else c for c in far]
        odd = [across(c, "narrow", narrow, 1) for c in far]
        pieces = [chunk, beside[:, start : start + rows]] + [piece for pair in zip(far, odd) for piece in pair]
        joint = 2 if mode == "relay" else 1
        sent = products(ids, pieces, kept, wide, joint)
        order = range(wide // joint - 1, 0, -1)
        given = [across(sent[k], "wide", wide, joint * k) for k in order] + [sent[0]]
        plan = [(i, joint * k, 0) for i, k in enumerate([*order, 0])]
        arrivals.append(given[:-1])
        if mode == "relay":
            size = given[0].shape[0] // 2
            passed = across(jnp.concatenate([g[size:] for g in given]), "wide", wide, 1)
            plan += [(len(given), (2 * k) ^ 1, i * size) for i, k in enumerate([*order, 0])]
            given.append(passed)
        received.append((given, tuple(plan)))
        ready = [sent[0]]
    held = None
    for (given, plan), start, rows in zip(received, starts, parts):
        held = summed(ids, targets, counts, given, plan, held, start, rows, cols, height)
    return held


def solution(mesh):
    in_specs = (P("narrow", "wide", None), P("wide", None, None, "narrow"), P(), P())
    out_specs = P("wide", None, "narrow")
    return jax.shard_map(
        on_device, mesh=mesh, in_specs=in_specs, out_specs=out_specs, check_vma=False
    )
```

```python
import functools

import jax
import jax.numpy as jnp
from jax import lax
from jax.experimental import pallas as pl
from jax.experimental.pallas import tpu as pltpu
from jax.sharding import PartitionSpec as P

MIB = 1 << 20
TOP = 32766.0
MANT = 8192.0
WORK = 16


def scale_code(peak):
    exponent = jnp.clip(jnp.floor(jnp.log2(jnp.maximum(peak, 1e-37))), -125.0, 125.0)
    mantissa = jnp.minimum(jnp.ceil(peak * jnp.exp2(-exponent) * MANT) + 1.0, 32000.0)
    return exponent, jnp.maximum(mantissa, 1.0)


def pick_kernel(start, source, *refs):
    out, done = refs[-2:]
    copy = pltpu.make_async_copy(source.at[:, pl.ds(start, out.shape[1]), :], out, done)
    copy.start()
    copy.wait()


def picked(source, start, rows, after):
    share, _, depth = source.shape
    return pl.pallas_call(
        functools.partial(pick_kernel, start),
        out_shape=jax.ShapeDtypeStruct((share, rows, depth), source.dtype),
        in_specs=[pl.BlockSpec(memory_space=pl.ANY)] * (1 + len(after)),
        out_specs=pl.BlockSpec(memory_space=pltpu.VMEM),
        scratch_shapes=[pltpu.SemaphoreType.DMA],
        compiler_params=pltpu.CompilerParams(vmem_limit_bytes=8 * MIB),
        name="picked_rows",
    )(source, *after)


def multiply_and_code(left, total, multiply, slots, cols, parts, put):
    height, lanes = sum(parts), cols // 128
    blocks = left.shape[0] // height

    lane = lax.broadcasted_iota(jnp.int32, (16, 128), 1)

    def one_slot(slot, codes):
        multiply(slot)
        codes = list(codes)
        for b in range(blocks):
            first = b * height
            for c, rows in enumerate(parts):
                for g in range(rows // 16):
                    value = total[first : first + 16, :]
                    first += 16
                    peak = jnp.max(jnp.abs(value), axis=1, keepdims=True)
                    exponent, mantissa = scale_code(peak)
                    value = value * jnp.exp2(-exponent) * (TOP * MANT / mantissa)
                    value = jnp.round(value).astype(jnp.int32).astype(jnp.int16)
                    at = (slot * (rows // 16) + g) * lanes
                    for t in range(lanes):
                        put(c, b, at + t, value[:, t * 128 : t * 128 + 128])
                    spot = (slot * (rows // 16) + g) * 2
                    code = codes[b * len(parts) + c]
                    code = jnp.where(lane == spot, exponent.astype(jnp.int32), code)
                    codes[b * len(parts) + c] = jnp.where(lane == spot + 1, mantissa.astype(jnp.int32), code)
        return tuple(codes)

    empty = tuple(jnp.zeros((16, 128), jnp.int32) for _ in range(blocks * len(parts)))
    codes = lax.fori_loop(0, slots, one_slot, empty)
    for b in range(blocks):
        for c, rows in enumerate(parts):
            put(c, b, slots * (rows // 16) * lanes, codes[b * len(parts) + c].astype(jnp.int16))


def stage_kernel(source, kept, done):
    copy = pltpu.make_async_copy(source, kept, done)
    copy.start()
    copy.wait()


def staged(integrals):
    return pl.pallas_call(
        stage_kernel,
        out_shape=pltpu.VMEM(integrals.shape, integrals.dtype),
        in_specs=[pl.BlockSpec(memory_space=pltpu.HBM)],
        out_specs=pl.BlockSpec(memory_space=pltpu.VMEM),
        scratch_shapes=[pltpu.SemaphoreType.DMA],
        compiler_params=pltpu.CompilerParams(vmem_limit_bytes=40 * MIB),
        name="staged_integrals",
    )(integrals)


def multiplied(left, kept, total):
    def multiply(slot):
        for n in range(0, kept.shape[3], 256):
            wide = slice(n, n + 256)
            total[:, wide] = jnp.dot(left[...], kept[0, slot, :, wide], preferred_element_type=jnp.float32)

    return multiply


def near_kernel(slots, share, waits, *refs):
    own, beside, kept, out, left, total = refs[waits:]
    rows = own.shape[1]
    for k, piece in enumerate((own, beside)):
        for sub in range(share):
            left[(k * share + sub) * rows : (k * share + sub + 1) * rows, :] = piece[sub]

    def put(c, b, tile, value):
        out[b, tile] = value

    multiply_and_code(left, total, multiplied(left, kept, total), slots, kept.shape[3], (rows,), put)


def far_kernel(slots, wide, count, share, rows, waits, early_count, ids, *refs):
    refs = refs[waits:]
    pieces, early, kept = refs[:count], refs[count : count + early_count], refs[count + early_count]
    outs = refs[count + early_count + 1 : -3]
    left, total, ready = refs[-3:]
    cols = kept.shape[3]
    me, mine = ids[0], ids[1]
    tiles = ready.shape[1]
    blocks = [(piece, at) for piece in pieces for at in range(piece.shape[0])]
    for b, (piece, at) in enumerate(blocks):
        left[b * rows : (b + 1) * rows, :] = piece[at]

    def place(k, sub):
        return ((mine ^ k) * share + sub) ^ me

    def put(c, b, tile, value):
        ready[place(2 * early_count + b // share, b % share), tile] = value

    for given in early:
        for b in range(given.shape[0]):
            ready[place(b // share, b % share)] = given[b]
    multiply_and_code(left, total, multiplied(left, kept, total), slots, cols, (rows,), put)
    for s in range(wide):
        outs[s][...] = ready[s]


def tile_count(slots, rows, cols):
    return slots * (rows // 16) * (cols // 128) + 1


def near_products(own, beside, integrals, after):
    _, slots, depth, cols = integrals.shape
    share, rows, _ = own.shape
    vmem = pl.BlockSpec(memory_space=pltpu.VMEM)
    return pl.pallas_call(
        functools.partial(near_kernel, slots, share, len(after)),
        out_shape=jax.ShapeDtypeStruct((2 * share, tile_count(slots, rows, cols), 16, 128), jnp.int16),
        in_specs=[pl.BlockSpec(memory_space=pl.ANY)] * len(after) + [vmem] * 3,
        out_specs=vmem,
        scratch_shapes=[
            pltpu.VMEM((2 * share * rows, depth), integrals.dtype),
            pltpu.VMEM((2 * share * rows, cols), jnp.float32),
        ],
        compiler_params=pltpu.CompilerParams(vmem_limit_bytes=16 * MIB),
        cost_estimate=pl.CostEstimate(
            flops=WORK * slots * 2 * share * rows * depth * cols,
            bytes_accessed=4 * share * rows * depth,
            transcendentals=0,
        ),
        name="near_products",
    )(*after, own, beside, integrals)


def far_products(ids, pieces, early, integrals, wide, share, after):
    _, slots, depth, cols = integrals.shape
    count, rows = len(pieces), pieces[0].shape[1]
    blocks = sum(piece.shape[0] for piece in pieces)
    tiles = tile_count(slots, rows, cols)
    vmem = pl.BlockSpec(memory_space=pltpu.VMEM)
    return pl.pallas_call(
        functools.partial(far_kernel, slots, wide, count, share, rows, len(after), len(early)),
        out_shape=[jax.ShapeDtypeStruct((tiles, 16, 128), jnp.int16)] * wide,
        in_specs=[pl.BlockSpec(memory_space=pltpu.SMEM)]
        + [pl.BlockSpec(memory_space=pl.ANY)] * len(after)
        + [vmem] * (count + len(early) + 1),
        out_specs=[vmem] * wide,
        scratch_shapes=[
            pltpu.VMEM((blocks * rows, depth), integrals.dtype),
            pltpu.VMEM((blocks * rows, cols), jnp.float32),
            pltpu.VMEM((wide, tiles, 16, 128), jnp.int16),
        ],
        compiler_params=pltpu.CompilerParams(vmem_limit_bytes=16 * MIB),
        cost_estimate=pl.CostEstimate(
            flops=WORK * slots * blocks * rows * depth * cols,
            bytes_accessed=2 * blocks * rows * depth,
            transcendentals=0,
        ),
        name="far_products",
    )(ids, *after, *pieces, *early, integrals)


def sum_kernel(slots, plan, start, rows, cols, ids, targets, counts, *refs):
    out, total, turned, done = refs[-4:]
    me = ids[0]
    groups, lanes = rows // 16, cols // 128
    tiles = slots * groups * lanes + 1
    total[...] = jnp.zeros_like(total)
    lane = lax.broadcasted_iota(jnp.int32, (16, 128), 1)
    for index, bits, at in plan:
        panel = me ^ bits
        codes = refs[index][at + tiles - 1].astype(jnp.int32)
        for j in range(slots):

            @pl.when(j < counts[panel])
            def add():
                tile = targets[panel * slots + j]
                for g in range(groups):
                    spot = (j * groups + g) * 2
                    exponent = jnp.sum(jnp.where(lane == spot, codes, 0).astype(jnp.float32), axis=1, keepdims=True)
                    mantissa = jnp.sum(jnp.where(lane == spot + 1, codes, 0).astype(jnp.float32), axis=1, keepdims=True)
                    scale = jnp.exp2(exponent) * (mantissa * (1.0 / (TOP * MANT)))
                    for t in range(lanes):
                        value = refs[index][at + (j * groups + g) * lanes + t].astype(jnp.int32).astype(jnp.float32)
                        total[tile, g * 16 : g * 16 + 16, t * 128 : t * 128 + 128] += value * scale
    copies = []
    for g in range(rows // 8):
        part = slice(g * 8, g * 8 + 8)
        for t in range(lanes):
            span = slice(t * 128, t * 128 + 128)
            turned[part, :, span] = jnp.swapaxes(total[:, part, span], 0, 1)
        copies.append(pltpu.make_async_copy(turned.at[part], out.at[pl.ds(start + g * 8, 8)], done.at[g]))
        copies[-1].start()
    for copy in copies:
        copy.wait()


def summed(ids, targets, counts, given, plan, held, start, rows, cols, height):
    pairs, slots = targets.shape
    extra = [] if held is None else [held]
    smem, vmem = pl.BlockSpec(memory_space=pltpu.SMEM), pl.BlockSpec(memory_space=pltpu.VMEM)
    return pl.pallas_call(
        functools.partial(sum_kernel, slots, plan, start, rows, cols),
        out_shape=jax.ShapeDtypeStruct((height, pairs, cols), jnp.float32),
        in_specs=[smem] * 3 + [vmem] * len(given) + [pl.BlockSpec(memory_space=pl.ANY)] * len(extra),
        out_specs=pl.BlockSpec(memory_space=pl.ANY),
        scratch_shapes=[
            pltpu.VMEM((pairs, rows, cols), jnp.float32),
            pltpu.VMEM((rows, pairs, cols), jnp.float32),
            pltpu.SemaphoreType.DMA((rows // 8,)),
        ],
        input_output_aliases={3 + len(given): 0} if extra else {},
        compiler_params=pltpu.CompilerParams(vmem_limit_bytes=32 * MIB),
        cost_estimate=pl.CostEstimate(
            flops=4 * pairs * slots * rows * cols,
            bytes_accessed=2 * pairs * slots * rows * cols + 4 * pairs * rows * cols,
            transcendentals=0,
        ),
        name="tile_sums",
    )(ids, targets.reshape(-1), counts, *given, *extra)


def on_device(amplitudes, integrals, targets, counts):
    wide, narrow = lax.axis_size("wide"), lax.axis_size("narrow")
    me, mine = lax.axis_index("wide"), lax.axis_index("narrow")
    ids = jnp.stack([me, mine]).astype(jnp.int32)
    depth, cols = integrals.shape[2], integrals.shape[3]
    share = wide // narrow
    height = amplitudes.shape[0] // share
    own = amplitudes.reshape(share, height, depth)
    parts = (height // 2, height - height // 2)

    def across(array, axis, size, bits):
        return lax.ppermute(array, axis, [(i, i ^ bits) for i in range(size)])

    starts = [sum(parts[:i]) for i in range(len(parts))]
    beside = across(own, "narrow", narrow, 1)
    kept = staged(integrals)
    both = jnp.concatenate([own[:, parts[0] :], beside[:, parts[0] :]])
    received, after, waits = [], [], []
    for start, rows in zip(starts, parts):
        chunk = picked(both, start - parts[0], rows, after) if start else picked(own, start, rows, after)
        far = [across(chunk, "narrow", narrow, k) for k in range(2, narrow, 2)]
        after = far[-1:]
        early = [near_products(own[:, start : start + rows], beside[:, start : start + rows], kept, waits)]
        if not start:
            odd = [across(picked(c, 0, rows, [kept, *early]), "narrow", narrow, 1) for c in far]
            pieces = [piece for pair in zip(far, odd) for piece in pair]
        else:
            pieces = far
        sent = far_products(ids, pieces, early, kept, wide, share, waits)
        waits = [sent[0]]
        crossing, others = [*range(wide // 2, wide)], [*range(2, wide // 2)]
        order = [1, *others[:1], *crossing, *others[1:]] if rows == height - start else [*crossing, 1, *others]
        given = [across(sent[s], "wide", wide, s) for s in order] + [sent[0]]
        received.append((given, tuple((i, s, 0) for i, s in enumerate([*order, 0]))))
    held = None
    for (given, plan), start, rows in zip(received, starts, parts):
        held = summed(ids, targets, counts, given, plan, held, start, rows, cols, height)
    return held


def solution(mesh):
    in_specs = (P("narrow", "wide", None), P("wide", None, None, "narrow"), P(), P())
    out_specs = P("wide", None, "narrow")
    return jax.shard_map(
        on_device, mesh=mesh, in_specs=in_specs, out_specs=out_specs, check_vma=False
    )
```

```python
import functools

import jax
import jax.numpy as jnp
from jax import lax
from jax.experimental import pallas as pl
from jax.experimental.pallas import tpu as pltpu
from jax.sharding import PartitionSpec as P

MIB = 1 << 20
TOP = 32766.0
MANT = 8192.0
WORK = 16


def scale_code(peak):
    exponent = jnp.clip(jnp.floor(jnp.log2(jnp.maximum(peak, 1e-37))), -125.0, 125.0)
    mantissa = jnp.minimum(jnp.ceil(peak * jnp.exp2(-exponent) * MANT) + 1.0, 32000.0)
    return exponent, jnp.maximum(mantissa, 1.0)


def pick_kernel(start, source, *refs):
    out, done = refs[-2:]
    copy = pltpu.make_async_copy(source.at[:, pl.ds(start, out.shape[1]), :], out, done)
    copy.start()
    copy.wait()


def picked(source, start, rows, after):
    share, _, depth = source.shape
    return pl.pallas_call(
        functools.partial(pick_kernel, start),
        out_shape=jax.ShapeDtypeStruct((share, rows, depth), source.dtype),
        in_specs=[pl.BlockSpec(memory_space=pl.ANY)] * (1 + len(after)),
        out_specs=pl.BlockSpec(memory_space=pltpu.VMEM),
        scratch_shapes=[pltpu.SemaphoreType.DMA],
        compiler_params=pltpu.CompilerParams(vmem_limit_bytes=8 * MIB),
        name="picked_rows",
    )(source, *after)


def multiply_and_code(left, total, multiply, slots, cols, parts, put):
    height, lanes = sum(parts), cols // 128
    blocks = left.shape[0] // height

    lane = lax.broadcasted_iota(jnp.int32, (16, 128), 1)

    def one_slot(slot, codes):
        multiply(slot)
        codes = list(codes)
        for b in range(blocks):
            first = b * height
            for c, rows in enumerate(parts):
                for g in range(rows // 16):
                    value = total[first : first + 16, :]
                    first += 16
                    peak = jnp.max(jnp.abs(value), axis=1, keepdims=True)
                    exponent, mantissa = scale_code(peak)
                    value = value * jnp.exp2(-exponent) * (TOP * MANT / mantissa)
                    value = jnp.round(value).astype(jnp.int32).astype(jnp.int16)
                    at = (slot * (rows // 16) + g) * lanes
                    for t in range(lanes):
                        put(c, b, at + t, value[:, t * 128 : t * 128 + 128])
                    spot = (slot * (rows // 16) + g) * 2
                    code = codes[b * len(parts) + c]
                    code = jnp.where(lane == spot, exponent.astype(jnp.int32), code)
                    codes[b * len(parts) + c] = jnp.where(lane == spot + 1, mantissa.astype(jnp.int32), code)
        return tuple(codes)

    empty = tuple(jnp.zeros((16, 128), jnp.int32) for _ in range(blocks * len(parts)))
    codes = lax.fori_loop(0, slots, one_slot, empty)
    for b in range(blocks):
        for c, rows in enumerate(parts):
            put(c, b, slots * (rows // 16) * lanes, codes[b * len(parts) + c].astype(jnp.int16))


def stage_kernel(source, kept, done):
    copy = pltpu.make_async_copy(source, kept, done)
    copy.start()
    copy.wait()


def staged(integrals):
    return pl.pallas_call(
        stage_kernel,
        out_shape=pltpu.VMEM(integrals.shape, integrals.dtype),
        in_specs=[pl.BlockSpec(memory_space=pltpu.HBM)],
        out_specs=pl.BlockSpec(memory_space=pltpu.VMEM),
        scratch_shapes=[pltpu.SemaphoreType.DMA],
        compiler_params=pltpu.CompilerParams(vmem_limit_bytes=40 * MIB),
        name="staged_integrals",
    )(integrals)


def multiplied(left, kept, total):
    def multiply(slot):
        for n in range(0, kept.shape[3], 256):
            wide = slice(n, n + 256)
            total[:, wide] = jnp.dot(left[...], kept[0, slot, :, wide], preferred_element_type=jnp.float32)

    return multiply


def near_kernel(slots, share, waits, *refs):
    own, beside, kept, out, left, total = refs[waits:]
    rows = own.shape[1]
    for k, piece in enumerate((own, beside)):
        for sub in range(share):
            left[(k * share + sub) * rows : (k * share + sub + 1) * rows, :] = piece[sub]

    def put(c, b, tile, value):
        out[b, tile] = value

    multiply_and_code(left, total, multiplied(left, kept, total), slots, kept.shape[3], (rows,), put)


def far_kernel(slots, wide, count, share, rows, waits, early_count, ids, *refs):
    refs = refs[waits:]
    pieces, early, kept = refs[:count], refs[count : count + early_count], refs[count + early_count]
    outs = refs[count + early_count + 1 : -3]
    left, total, ready = refs[-3:]
    cols = kept.shape[3]
    me, mine = ids[0], ids[1]
    tiles = ready.shape[1]
    blocks = [(piece, at) for piece in pieces for at in range(piece.shape[0])]
    for b, (piece, at) in enumerate(blocks):
        left[b * rows : (b + 1) * rows, :] = piece[at]

    def place(k, sub):
        return ((mine ^ k) * share + sub) ^ me

    def put(c, b, tile, value):
        ready[place(2 * early_count + b // share, b % share), tile] = value

    for given in early:
        for b in range(given.shape[0]):
            ready[place(b // share, b % share)] = given[b]
    multiply_and_code(left, total, multiplied(left, kept, total), slots, cols, (rows,), put)
    for s in range(wide):
        outs[s][...] = ready[s]


def tile_count(slots, rows, cols):
    return slots * (rows // 16) * (cols // 128) + 1


def near_products(own, beside, integrals, after):
    _, slots, depth, cols = integrals.shape
    share, rows, _ = own.shape
    vmem = pl.BlockSpec(memory_space=pltpu.VMEM)
    return pl.pallas_call(
        functools.partial(near_kernel, slots, share, len(after)),
        out_shape=jax.ShapeDtypeStruct((2 * share, tile_count(slots, rows, cols), 16, 128), jnp.int16),
        in_specs=[pl.BlockSpec(memory_space=pl.ANY)] * len(after) + [vmem] * 3,
        out_specs=vmem,
        scratch_shapes=[
            pltpu.VMEM((2 * share * rows, depth), integrals.dtype),
            pltpu.VMEM((2 * share * rows, cols), jnp.float32),
        ],
        compiler_params=pltpu.CompilerParams(vmem_limit_bytes=16 * MIB),
        cost_estimate=pl.CostEstimate(
            flops=WORK * slots * 2 * share * rows * depth * cols,
            bytes_accessed=4 * share * rows * depth,
            transcendentals=0,
        ),
        name="near_products",
    )(*after, own, beside, integrals)


def far_products(ids, pieces, early, integrals, wide, share, after):
    _, slots, depth, cols = integrals.shape
    count, rows = len(pieces), pieces[0].shape[1]
    blocks = sum(piece.shape[0] for piece in pieces)
    tiles = tile_count(slots, rows, cols)
    vmem = pl.BlockSpec(memory_space=pltpu.VMEM)
    return pl.pallas_call(
        functools.partial(far_kernel, slots, wide, count, share, rows, len(after), len(early)),
        out_shape=[jax.ShapeDtypeStruct((tiles, 16, 128), jnp.int16)] * wide,
        in_specs=[pl.BlockSpec(memory_space=pltpu.SMEM)]
        + [pl.BlockSpec(memory_space=pl.ANY)] * len(after)
        + [vmem] * (count + len(early) + 1),
        out_specs=[vmem] * wide,
        scratch_shapes=[
            pltpu.VMEM((blocks * rows, depth), integrals.dtype),
            pltpu.VMEM((blocks * rows, cols), jnp.float32),
            pltpu.VMEM((wide, tiles, 16, 128), jnp.int16),
        ],
        compiler_params=pltpu.CompilerParams(vmem_limit_bytes=16 * MIB),
        cost_estimate=pl.CostEstimate(
            flops=WORK * slots * blocks * rows * depth * cols,
            bytes_accessed=2 * blocks * rows * depth,
            transcendentals=0,
        ),
        name="far_products",
    )(ids, *after, *pieces, *early, integrals)


def sum_kernel(slots, plan, start, rows, cols, begun, last, ids, targets, counts, *refs):
    out, total, turned, done = refs[-4:] if last else (None, refs[-1], None, None)
    me = ids[0]
    groups, lanes = rows // 16, cols // 128
    tiles = slots * groups * lanes + 1
    total[...] = refs[len(plan)][...] if begun else jnp.zeros_like(total)
    scales = []
    for index, _, at in plan:
        codes = refs[index][at + tiles - 1].astype(jnp.int32).astype(jnp.float32)
        exponents = jnp.exp2(jnp.clip(codes, -125.0, 125.0))
        scales.append(exponents * (pltpu.roll(codes, 127, 1) * (1.0 / (TOP * MANT))))
    for (index, bits, at), scale in zip(plan, scales):
        panel = me ^ bits
        for j in range(slots):

            @pl.when(j < counts[panel])
            def add():
                tile = targets[panel * slots + j]
                spots = [(slice(g * 16, g * 16 + 16), slice(t * 128, t * 128 + 128)) for g in range(groups) for t in range(lanes)]
                columns = [scale[:, (j * groups + g) * 2 : (j * groups + g) * 2 + 1] for g in range(groups)]
                values = []
                for i, (r, c) in enumerate(spots):
                    value = refs[index][at + j * groups * lanes + i].astype(jnp.int32).astype(jnp.float32)
                    values.append(total[tile, r, c] + value * columns[i // lanes])
                for value, (r, c) in zip(values, spots):
                    total[tile, r, c] = value

    if not last:
        return
    copies = []
    for g in range(rows // 8):
        part = slice(g * 8, g * 8 + 8)
        for t in range(lanes):
            span = slice(t * 128, t * 128 + 128)
            turned[part, :, span] = jnp.swapaxes(total[:, part, span], 0, 1)
        copies.append(pltpu.make_async_copy(turned.at[part], out.at[pl.ds(start + g * 8, 8)], done.at[g]))
        copies[-1].start()
    for copy in copies:
        copy.wait()


def summed(ids, targets, counts, given, plan, begun, held, last, start, rows, cols, height):
    pairs, slots = targets.shape
    smem, vmem = pl.BlockSpec(memory_space=pltpu.SMEM), pl.BlockSpec(memory_space=pltpu.VMEM)
    scratch = [
        pltpu.VMEM((pairs, rows, cols), jnp.float32),
        pltpu.VMEM((rows, pairs, cols), jnp.float32),
        pltpu.SemaphoreType.DMA((rows // 8,)),
    ]
    shape = (height, pairs, cols) if last else (pairs, rows, cols)
    return pl.pallas_call(
        functools.partial(sum_kernel, slots, plan, start, rows, cols, len(begun) > 0, last),
        out_shape=jax.ShapeDtypeStruct(shape, jnp.float32),
        in_specs=[smem] * 3 + [vmem] * (len(given) + len(begun)) + [pl.BlockSpec(memory_space=pl.ANY)] * len(held),
        out_specs=pl.BlockSpec(memory_space=pl.ANY) if last else vmem,
        scratch_shapes=scratch if last else [],
        input_output_aliases={3 + len(given) + len(begun): 0} if held else {},
        compiler_params=pltpu.CompilerParams(vmem_limit_bytes=32 * MIB),
        cost_estimate=pl.CostEstimate(
            flops=4 * len(given) * slots * rows * cols,
            bytes_accessed=2 * len(given) * slots * rows * cols + 4 * pairs * rows * cols,
            transcendentals=0,
        ),
        name="tile_sums",
    )(ids, targets.reshape(-1), counts, *given, *begun, *held)


def on_device(amplitudes, integrals, targets, counts):
    wide, narrow = lax.axis_size("wide"), lax.axis_size("narrow")
    me, mine = lax.axis_index("wide"), lax.axis_index("narrow")
    ids = jnp.stack([me, mine]).astype(jnp.int32)
    depth, cols = integrals.shape[2], integrals.shape[3]
    share = wide // narrow
    height = amplitudes.shape[0] // share
    own = amplitudes.reshape(share, height, depth)
    parts = (height // 2, height - height // 2)

    def across(array, axis, size, bits):
        return lax.ppermute(array, axis, [(i, i ^ bits) for i in range(size)])

    starts = [sum(parts[:i]) for i in range(len(parts))]
    beside = across(own, "narrow", narrow, 1)
    kept = staged(integrals)
    both = jnp.concatenate([own[:, parts[0] :], beside[:, parts[0] :]])
    received, after, waits = [], [], []
    for start, rows in zip(starts, parts):
        chunk = picked(both, start - parts[0], rows, after) if start else picked(own, start, rows, after)
        far = [across(chunk, "narrow", narrow, k) for k in range(2, narrow, 2)]
        after = far[-1:]
        early = [near_products(own[:, start : start + rows], beside[:, start : start + rows], kept, waits)]
        if not start:
            odd = [across(picked(c, 0, rows, [kept, *early]), "narrow", narrow, 1) for c in far]
            pieces = [piece for pair in zip(far, odd) for piece in pair]
        else:
            pieces = far
        sent = far_products(ids, pieces, early, kept, wide, share, waits)
        waits = [sent[0]]
        crossing, others = [*range(wide // 2, wide)], [*range(2, wide // 2)]
        order = [*crossing, 1, *others]
        if start:
            order = [crossing[0], 1, crossing[1], *others[:1], *crossing[2:], *others[1:]]
        given = [across(sent[s], "wide", wide, s) for s in order] + [sent[0]]
        received.append((given, tuple((i, s, 0) for i, s in enumerate([*order, 0]))))
    held = []
    for (given, plan), start, rows in zip(received, starts, parts):
        begun = []
        if start:
            ahead = wide // 2
            first = [*given[:ahead], given[-1]]
            order = [s for _, s, _ in plan]
            marks = [*order[:ahead], 0]
            begun = [
                summed(ids, targets, counts, first, tuple((i, s, 0) for i, s in enumerate(marks)), [], [], False, start, rows, cols, height)
            ]
            given, marks = given[ahead:-1], order[ahead:-1]
            plan = tuple((i, s, 0) for i, s in enumerate(marks))
        held = [summed(ids, targets, counts, given, plan, begun, held, True, start, rows, cols, height)]
    return held[0]


def solution(mesh):
    in_specs = (P("narrow", "wide", None), P("wide", None, None, "narrow"), P(), P())
    out_specs = P("wide", None, "narrow")
    return jax.shard_map(
        on_device, mesh=mesh, in_specs=in_specs, out_specs=out_specs, check_vma=False
    )
```

```python
import functools

import jax
import jax.numpy as jnp
from jax import lax
from jax.experimental import pallas as pl
from jax.experimental.pallas import tpu as pltpu
from jax.sharding import PartitionSpec as P

MIB = 1 << 20
TOP = 32766.0
MANT = 8192.0
WORK = 16


def scale_code(peak):
    exponent = jnp.clip(jnp.floor(jnp.log2(jnp.maximum(peak, 1e-37))), -125.0, 125.0)
    mantissa = jnp.minimum(jnp.ceil(peak * jnp.exp2(-exponent) * MANT) + 1.0, 32000.0)
    return exponent, jnp.maximum(mantissa, 1.0)


def pick_kernel(start, source, *refs):
    out, done = refs[-2:]
    copy = pltpu.make_async_copy(source.at[:, pl.ds(start, out.shape[1]), :], out, done)
    copy.start()
    copy.wait()


def picked(source, start, rows, after):
    share, _, depth = source.shape
    return pl.pallas_call(
        functools.partial(pick_kernel, start),
        out_shape=jax.ShapeDtypeStruct((share, rows, depth), source.dtype),
        in_specs=[pl.BlockSpec(memory_space=pl.ANY)] * (1 + len(after)),
        out_specs=pl.BlockSpec(memory_space=pltpu.VMEM),
        scratch_shapes=[pltpu.SemaphoreType.DMA],
        compiler_params=pltpu.CompilerParams(vmem_limit_bytes=8 * MIB),
        name="picked_rows",
    )(source, *after)


def multiply_and_code(left, total, multiply, slots, cols, parts, put):
    height, lanes = sum(parts), cols // 128
    blocks = left.shape[0] // height

    lane = lax.broadcasted_iota(jnp.int32, (16, 128), 1)

    def one_slot(slot, codes):
        codes = list(codes)
        for b in range(blocks):
            first = b * height
            for c, rows in enumerate(parts):
                for g in range(rows // 16):
                    value = total[slot, first : first + 16, :]
                    first += 16
                    peak = jnp.max(jnp.abs(value), axis=1, keepdims=True)
                    exponent, mantissa = scale_code(peak)
                    value = value * jnp.exp2(-exponent) * (TOP * MANT / mantissa)
                    value = jnp.round(value).astype(jnp.int32).astype(jnp.int16)
                    at = (slot * (rows // 16) + g) * lanes
                    for t in range(lanes):
                        put(c, b, at + t, value[:, t * 128 : t * 128 + 128])
                    spot = (slot * (rows // 16) + g) * 2
                    code = codes[b * len(parts) + c]
                    code = jnp.where(lane == spot, exponent.astype(jnp.int32), code)
                    codes[b * len(parts) + c] = jnp.where(lane == spot + 1, mantissa.astype(jnp.int32), code)
        return tuple(codes)

    codes = tuple(jnp.zeros((16, 128), jnp.int32) for _ in range(blocks * len(parts)))
    multiply(0)
    for slot in range(slots):
        if slot + 1 < slots:
            multiply(slot + 1)
        codes = one_slot(slot, codes)
    for b in range(blocks):
        for c, rows in enumerate(parts):
            put(c, b, slots * (rows // 16) * lanes, codes[b * len(parts) + c].astype(jnp.int16))


def stage_kernel(source, kept, done):
    copy = pltpu.make_async_copy(source, kept, done)
    copy.start()
    copy.wait()


def staged(integrals):
    return pl.pallas_call(
        stage_kernel,
        out_shape=pltpu.VMEM(integrals.shape, integrals.dtype),
        in_specs=[pl.BlockSpec(memory_space=pltpu.HBM)],
        out_specs=pl.BlockSpec(memory_space=pltpu.VMEM),
        scratch_shapes=[pltpu.SemaphoreType.DMA],
        compiler_params=pltpu.CompilerParams(vmem_limit_bytes=40 * MIB),
        name="staged_integrals",
    )(integrals)


def multiplied(left, kept, total):
    def multiply(slot):
        for n in range(0, kept.shape[3], 256):
            wide = slice(n, n + 256)
            total[slot, :, wide] = jnp.dot(left[...], kept[0, slot, :, wide], preferred_element_type=jnp.float32)

    return multiply


def near_kernel(slots, share, waits, *refs):
    own, beside, kept, out, left, total = refs[waits:]
    rows = own.shape[1]
    for k, piece in enumerate((own, beside)):
        for sub in range(share):
            left[(k * share + sub) * rows : (k * share + sub + 1) * rows, :] = piece[sub]

    def put(c, b, tile, value):
        out[b, tile] = value

    multiply_and_code(left, total, multiplied(left, kept, total), slots, kept.shape[3], (rows,), put)


def far_kernel(slots, wide, count, share, rows, waits, early_count, ids, *refs):
    refs = refs[waits:]
    pieces, early, kept = refs[:count], refs[count : count + early_count], refs[count + early_count]
    outs = refs[count + early_count + 1 : -3]
    left, total, ready = refs[-3:]
    cols = kept.shape[3]
    me, mine = ids[0], ids[1]
    tiles = ready.shape[1]
    blocks = [(piece, at) for piece in pieces for at in range(piece.shape[0])]
    for b, (piece, at) in enumerate(blocks):
        left[b * rows : (b + 1) * rows, :] = piece[at]

    def place(k, sub):
        return ((mine ^ k) * share + sub) ^ me

    def put(c, b, tile, value):
        ready[place(2 * early_count + b // share, b % share), tile] = value

    for given in early:
        for b in range(given.shape[0]):
            ready[place(b // share, b % share)] = given[b]
    multiply_and_code(left, total, multiplied(left, kept, total), slots, cols, (rows,), put)
    for s in range(wide):
        outs[s][...] = ready[s]


def tile_count(slots, rows, cols):
    return slots * (rows // 16) * (cols // 128) + 1


def near_products(own, beside, integrals, after):
    _, slots, depth, cols = integrals.shape
    share, rows, _ = own.shape
    vmem = pl.BlockSpec(memory_space=pltpu.VMEM)
    return pl.pallas_call(
        functools.partial(near_kernel, slots, share, len(after)),
        out_shape=jax.ShapeDtypeStruct((2 * share, tile_count(slots, rows, cols), 16, 128), jnp.int16),
        in_specs=[pl.BlockSpec(memory_space=pl.ANY)] * len(after) + [vmem] * 3,
        out_specs=vmem,
        scratch_shapes=[
            pltpu.VMEM((2 * share * rows, depth), integrals.dtype),
            pltpu.VMEM((slots, 2 * share * rows, cols), jnp.float32),
        ],
        compiler_params=pltpu.CompilerParams(vmem_limit_bytes=16 * MIB),
        cost_estimate=pl.CostEstimate(
            flops=WORK * slots * 2 * share * rows * depth * cols,
            bytes_accessed=4 * share * rows * depth,
            transcendentals=0,
        ),
        name="near_products",
    )(*after, own, beside, integrals)


def far_products(ids, pieces, early, integrals, wide, share, after):
    _, slots, depth, cols = integrals.shape
    count, rows = len(pieces), pieces[0].shape[1]
    blocks = sum(piece.shape[0] for piece in pieces)
    tiles = tile_count(slots, rows, cols)
    vmem = pl.BlockSpec(memory_space=pltpu.VMEM)
    return pl.pallas_call(
        functools.partial(far_kernel, slots, wide, count, share, rows, len(after), len(early)),
        out_shape=[jax.ShapeDtypeStruct((tiles, 16, 128), jnp.int16)] * wide,
        in_specs=[pl.BlockSpec(memory_space=pltpu.SMEM)]
        + [pl.BlockSpec(memory_space=pl.ANY)] * len(after)
        + [vmem] * (count + len(early) + 1),
        out_specs=[vmem] * wide,
        scratch_shapes=[
            pltpu.VMEM((blocks * rows, depth), integrals.dtype),
            pltpu.VMEM((slots, blocks * rows, cols), jnp.float32),
            pltpu.VMEM((wide, tiles, 16, 128), jnp.int16),
        ],
        compiler_params=pltpu.CompilerParams(vmem_limit_bytes=16 * MIB),
        cost_estimate=pl.CostEstimate(
            flops=WORK * slots * blocks * rows * depth * cols,
            bytes_accessed=2 * blocks * rows * depth,
            transcendentals=0,
        ),
        name="far_products",
    )(ids, *after, *pieces, *early, integrals)


def sum_kernel(slots, plan, start, rows, cols, begun, last, ids, targets, counts, *refs):
    out, total, turned, done = refs[-4:] if last else (None, refs[-1], None, None)
    me = ids[0]
    groups, lanes = rows // 16, cols // 128
    tiles = slots * groups * lanes + 1
    total[...] = refs[len(plan)][...] if begun else jnp.zeros_like(total)
    scales = []
    for index, _, at in plan:
        codes = refs[index][at + tiles - 1].astype(jnp.int32).astype(jnp.float32)
        exponents = jnp.exp2(jnp.clip(codes, -125.0, 125.0))
        scales.append(exponents * (pltpu.roll(codes, 127, 1) * (1.0 / (TOP * MANT))))
    for (index, bits, at), scale in zip(plan, scales):
        panel = me ^ bits
        for j in range(slots):

            @pl.when(j < counts[panel])
            def add():
                tile = targets[panel * slots + j]
                spots = [(slice(g * 16, g * 16 + 16), slice(t * 128, t * 128 + 128)) for g in range(groups) for t in range(lanes)]
                columns = [scale[:, (j * groups + g) * 2 : (j * groups + g) * 2 + 1] for g in range(groups)]
                values = []
                for i, (r, c) in enumerate(spots):
                    value = refs[index][at + j * groups * lanes + i].astype(jnp.int32).astype(jnp.float32)
                    values.append(total[tile, r, c] + value * columns[i // lanes])
                for value, (r, c) in zip(values, spots):
                    total[tile, r, c] = value

    if not last:
        return
    copies = []
    for g in range(rows // 8):
        part = slice(g * 8, g * 8 + 8)
        for t in range(lanes):
            span = slice(t * 128, t * 128 + 128)
            turned[part, :, span] = jnp.swapaxes(total[:, part, span], 0, 1)
        copies.append(pltpu.make_async_copy(turned.at[part], out.at[pl.ds(start + g * 8, 8)], done.at[g]))
        copies[-1].start()
    for copy in copies:
        copy.wait()


def summed(ids, targets, counts, given, plan, begun, held, last, start, rows, cols, height):
    pairs, slots = targets.shape
    smem, vmem = pl.BlockSpec(memory_space=pltpu.SMEM), pl.BlockSpec(memory_space=pltpu.VMEM)
    scratch = [
        pltpu.VMEM((pairs, rows, cols), jnp.float32),
        pltpu.VMEM((rows, pairs, cols), jnp.float32),
        pltpu.SemaphoreType.DMA((rows // 8,)),
    ]
    shape = (height, pairs, cols) if last else (pairs, rows, cols)
    return pl.pallas_call(
        functools.partial(sum_kernel, slots, plan, start, rows, cols, len(begun) > 0, last),
        out_shape=jax.ShapeDtypeStruct(shape, jnp.float32),
        in_specs=[smem] * 3 + [vmem] * (len(given) + len(begun)) + [pl.BlockSpec(memory_space=pl.ANY)] * len(held),
        out_specs=pl.BlockSpec(memory_space=pl.ANY) if last else vmem,
        scratch_shapes=scratch if last else [],
        input_output_aliases={3 + len(given) + len(begun): 0} if held else {},
        compiler_params=pltpu.CompilerParams(vmem_limit_bytes=32 * MIB),
        cost_estimate=pl.CostEstimate(
            flops=4 * len(given) * slots * rows * cols,
            bytes_accessed=2 * len(given) * slots * rows * cols + 4 * pairs * rows * cols,
            transcendentals=0,
        ),
        name="tile_sums",
    )(ids, targets.reshape(-1), counts, *given, *begun, *held)


def on_device(amplitudes, integrals, targets, counts):
    wide, narrow = lax.axis_size("wide"), lax.axis_size("narrow")
    me, mine = lax.axis_index("wide"), lax.axis_index("narrow")
    ids = jnp.stack([me, mine]).astype(jnp.int32)
    depth, cols = integrals.shape[2], integrals.shape[3]
    share = wide // narrow
    height = amplitudes.shape[0] // share
    own = amplitudes.reshape(share, height, depth)
    parts = (height // 2, height - height // 2)

    def across(array, axis, size, bits):
        return lax.ppermute(array, axis, [(i, i ^ bits) for i in range(size)])

    starts = [sum(parts[:i]) for i in range(len(parts))]
    beside = across(own, "narrow", narrow, 1)
    kept = staged(integrals)
    both = jnp.concatenate([own[:, parts[0] :], beside[:, parts[0] :]])
    received, after, waits = [], [], []
    for start, rows in zip(starts, parts):
        chunk = picked(both, start - parts[0], rows, after) if start else picked(own, start, rows, after)
        far = [across(chunk, "narrow", narrow, k) for k in range(2, narrow, 2)]
        after = far[-1:]
        early = [near_products(own[:, start : start + rows], beside[:, start : start + rows], kept, waits)]
        if not start:
            odd = [across(picked(c, 0, rows, [kept, *early]), "narrow", narrow, 1) for c in far]
            pieces = [piece for pair in zip(far, odd) for piece in pair]
        else:
            pieces = far
        sent = far_products(ids, pieces, early, kept, wide, share, waits)
        waits = [sent[0]]
        crossing, others = [*range(wide // 2, wide)], [*range(2, wide // 2)]
        order = [*crossing, 1, *others]
        if start:
            order = [crossing[0], 1, crossing[1], *others[:1], *crossing[2:], *others[1:]]
        given = [across(sent[s], "wide", wide, s) for s in order] + [sent[0]]
        received.append((given, tuple((i, s, 0) for i, s in enumerate([*order, 0]))))
    held = []
    for (given, plan), start, rows in zip(received, starts, parts):
        begun = []
        if start:
            ahead = wide // 2
            first = [*given[:ahead], given[-1]]
            order = [s for _, s, _ in plan]
            marks = [*order[:ahead], 0]
            begun = [
                summed(ids, targets, counts, first, tuple((i, s, 0) for i, s in enumerate(marks)), [], [], False, start, rows, cols, height)
            ]
            given, marks = given[ahead:-1], order[ahead:-1]
            plan = tuple((i, s, 0) for i, s in enumerate(marks))
        held = [summed(ids, targets, counts, given, plan, begun, held, True, start, rows, cols, height)]
    return held[0]


def solution(mesh):
    in_specs = (P("narrow", "wide", None), P("wide", None, None, "narrow"), P(), P())
    out_specs = P("wide", None, "narrow")
    return jax.shard_map(
        on_device, mesh=mesh, in_specs=in_specs, out_specs=out_specs, check_vma=False
    )
```
